128 devices in a mesh: owner: 8 (over x_hi, y), batch: 16 (over x_lo, z, core).
Axes of the slice: x: 4 (x_hi: 2, x_lo: 2; x = x_hi * 2 + x_lo), y: 4, z: 4, core: 2. Of those that a mesh axis runs over, the one named last changes fastest.
Arguments:
- hidden: bfloat16 [2048, 6144], P(('owner', 'batch')), may hold values from -6 to 6
- gains: float32 [2, 6144], replicated, may hold values from 0.25 to 1.75
- up_rows: bfloat16 [98304, 6144], P(('owner', 'batch')), may hold values from -0.078125 to 0.078125
- down_rows: bfloat16 [98304, 6144], P(('owner', 'batch')), may hold values from -0.09375 to 0.09375
- pick: int32 [8, 128], replicated, may hold values from 0 to 6, as said below
Outputs:
- final_rows: bfloat16 [2048, 6144], P(('owner', 'batch'))
The draws below stay inside these ranges and needn't reach their ends.
Inputs may be any that keep to these rules, and one draw needn't show every extreme that they name: pick[g, u] names the one block among unit u's 6 blocks that row block g uses, or is 6 when it uses none of them. In every row block there is a lane of which every unit is used, and a unit that is not.
All inputs are finite; a program needn't handle non-finite values.
Results may differ from the reference program's by a relative error of at most 0.018.
Values may be sent and summed in bfloat16 or wider, within the bound.
No kernel may reach another device: no remote copies, remote signals or barrier semaphores. Data moves between devices by JAX's collectives and lax.ppermute only.
A program may use at most 192 MiB of HBM per device.

```python
import jax
import jax.numpy as jnp
from jax import lax

D = 6144
FF = 49152
BLOCK = 128
LAYERS = 2
HELD = 6
GROUP_ROWS = 256
REQUESTS = 2048
N_OWNER = 8
N_BATCH = 16
DEVICES = 128


def draw_pick(key, part):
    keys = jax.random.split(jax.random.fold_in(key, 17), 5)
    level = jax.random.randint(keys[0], (N_OWNER, 1), 1, 10)
    roll = jax.random.randint(keys[1], (N_OWNER, DEVICES), 0, 10)
    which = jax.random.randint(keys[2], (N_OWNER, DEVICES), 0, HELD)
    chosen = jnp.where(roll < level, which, HELD)
    unit_ids = jnp.arange(DEVICES)[None, :]
    full_lane = jax.random.randint(keys[3], (N_OWNER, 1), 0, N_BATCH)
    chosen = jnp.where(unit_ids % N_BATCH == full_lane, which, chosen)
    empty_lane = (full_lane + 1 + jax.random.randint(keys[4], (N_OWNER, 1), 0, N_BATCH - 1)) % N_BATCH
    chosen = jnp.where(unit_ids == empty_lane, HELD, chosen)
    return chosen.astype(jnp.int32)


def level_of(stream_key, shape, cuts, least, largest):
    gain, own = 1.0, jax.random.fold_in(stream_key, 6)
    for dim, parts in cuts:
        heights = jnp.exp(jax.random.uniform(jax.random.fold_in(own, dim), (parts,), jnp.float32, least / len(cuts), largest / len(cuts)))
        gain = gain * jnp.repeat(heights, shape[dim] // parts).reshape([-1 if axis == dim else 1 for axis in range(len(shape))])
    return gain


def bell_draw(own_key, dims, scale, most, cuts=(), dtype=jnp.bfloat16):
    level = level_of(own_key, dims, cuts, -0.22, 0.18) if cuts else 1.0
    entries = jax.random.normal(own_key, dims, jnp.float32) * scale * level
    return jnp.minimum(jnp.maximum(entries, -most), most).astype(dtype)


def setup_inputs(seed: int = 0) -> dict:
    key_list = jax.random.split(jax.random.key(seed), 6)
    hidden = bell_draw(key_list[0], (REQUESTS, D), 1.0, 6.0, ((0, 128),))
    gains = jnp.clip(1.0 + 0.15 * jax.random.normal(key_list[1], (LAYERS, D), jnp.float32), 0.25, 1.75)
    up_rows = bell_draw(key_list[2], (LAYERS * FF, D), D ** -0.5, 0.078125, ((0, 128),))
    down_rows = bell_draw(key_list[3], (LAYERS * FF, D), (DEVICES * BLOCK // 4) ** -0.5, 0.09375, ((0, 128),))
    pick = draw_pick(jax.random.fold_in(key_list[5], 71), 0)
    return {"hidden": hidden, "gains": gains, "up_rows": up_rows, "down_rows": down_rows, "pick": pick}


def normalize(rows_in, gain_row):
    values = rows_in.astype(jnp.float32)
    row_mean = lax.optimization_barrier(jnp.mean(values, axis=1, keepdims=True))
    centered = values - row_mean
    row_var = lax.optimization_barrier(jnp.mean(centered * centered, axis=1, keepdims=True))
    return (centered * lax.rsqrt(row_var + 1e-05) * gain_row[None, :]).astype(jnp.bfloat16)

def reference(hidden, gains, up_rows, down_rows, pick):
    dev_layer = DEVICES // LAYERS
    up_stack = up_rows.reshape(DEVICES * HELD, BLOCK, D)
    down_stack = down_rows.reshape(DEVICES * HELD, BLOCK, D)
    state = hidden
    for layer_at in range(LAYERS):
        normed = normalize(state, gains[layer_at])
        pieces = []
        for group_at in range(N_OWNER):
            units = (layer_at * dev_layer + jnp.arange(dev_layer)).astype(jnp.int32)
            chosen = pick[group_at, units]
            live_units = (chosen < HELD).astype(jnp.float32)
            selected = (units * HELD + jnp.minimum(chosen, HELD - 1)).astype(jnp.int32)
            up_sel = up_stack[selected].reshape(dev_layer * BLOCK, D)
            down_sel = down_stack[selected].astype(jnp.float32)
            group_rows = normed[group_at * GROUP_ROWS:(group_at + 1) * GROUP_ROWS]
            pre_act = jnp.dot(group_rows, up_sel.T, preferred_element_type=jnp.float32)
            neuron_mask = jnp.repeat(live_units, BLOCK)
            active = (jnp.maximum(pre_act, 0.0) * neuron_mask[None, :]).astype(jnp.bfloat16)
            active_four = active.astype(jnp.float32).reshape(GROUP_ROWS, dev_layer // N_BATCH, N_BATCH, BLOCK)
            down_four = down_sel.reshape(dev_layer // N_BATCH, N_BATCH, BLOCK, D)
            lane_terms = jnp.einsum('rjbk,jbkd->brd', active_four, down_four)
            lane_sum = lax.optimization_barrier(lane_terms.astype(jnp.bfloat16))
            pieces.append(lax.optimization_barrier(jnp.sum(lane_sum.astype(jnp.float32), axis=0)))
        update = jnp.concatenate(pieces, axis=0)
        state = (state.astype(jnp.float32) + update).astype(jnp.bfloat16)
    return state
```

```python
import jax
import jax.numpy as jnp
from jax import lax
from jax.experimental import pallas as pl
from jax.experimental.pallas import tpu as pltpu
from jax.sharding import Mesh
from jax.sharding import PartitionSpec as P

BLOCK = 128
LAYERS = 2
HELD = 6
ROW = ("xl", "z", "c")
SWAP = [(0, 1), (1, 0)]


def normalize(rows_in, gain_row):
    values = rows_in.astype(jnp.float32)
    row_mean = jnp.mean(values, axis=1, keepdims=True)
    centered = values - row_mean
    row_var = jnp.mean(centered * centered, axis=1, keepdims=True)
    return (centered * lax.rsqrt(row_var + 1e-05) * gain_row[None, :]).astype(jnp.bfloat16)


def pick_blocks(chosen, rows):
    groups = chosen.shape[0]
    half = rows.shape[1] // 2

    def copy(chosen_ref, in_ref, out_ref):
        out_ref[0] = in_ref[...]

    return pl.pallas_call(
        copy,
        grid_spec=pltpu.PrefetchScalarGridSpec(
            num_scalar_prefetch=1,
            grid=(groups, 2),
            in_specs=[pl.BlockSpec((BLOCK, half), lambda g, h, ch: (ch[g], h))],
            out_specs=pl.BlockSpec((1, BLOCK, half), lambda g, h, ch: (g * 2 + h, 0, 0)),
        ),
        out_shape=jax.ShapeDtypeStruct((groups * 2, BLOCK, half), rows.dtype),
        cost_estimate=pl.CostEstimate(flops=0, bytes_accessed=groups * BLOCK * half * 8, transcendentals=0),
        name="pick_blocks",
    )(chosen, rows)


def body(hidden, gains, up_rows, down_rows, pick):
    owners, lanes = 8, 16
    owner = lax.axis_index(("xh", "y"))
    chip_lane = lax.axis_index(("xl", "z")) * 2
    core = lax.axis_index("c")
    local_rows, width = hidden.shape
    half = width // 2
    my_picks = lax.dynamic_slice_in_dim(pick, owner * lanes + chip_lane + core, 1, 1)[:, 0]
    chosen = jnp.minimum(my_picks, HELD - 1)
    group_picks = lax.dynamic_slice_in_dim(pick, owner, 1, 0).reshape(owners, lanes)
    pair_picks = lax.dynamic_slice_in_dim(group_picks, chip_lane, 2, 1)
    live = (pair_picks < HELD).astype(jnp.float32).reshape(LAYERS, owners // LAYERS * 2)

    up_all = lax.all_to_all(pick_blocks(chosen, up_rows), ("xh", "y", "c"), 0, 0, tiled=True)
    down_all = lax.all_to_all(pick_blocks(chosen, down_rows), ("xh", "y", "c"), 0, 0, tiled=True)
    per_layer = owners // LAYERS * 2
    up_all = up_all.reshape(LAYERS, per_layer * BLOCK, half)
    down_all = down_all.reshape(LAYERS, per_layer * BLOCK, half)

    residual = hidden
    for layer_at in range(LAYERS):
        normed = normalize(residual, gains[layer_at])
        halves = jnp.stack([normed[:, :half], normed[:, half:]])
        if layer_at == 0:
            mine = lax.dynamic_index_in_dim(halves, core, 0, keepdims=False)
            other = lax.dynamic_index_in_dim(halves, 1 - core, 0, keepdims=False)
            got = lax.ppermute(other, "c", SWAP)
            both = jnp.where(core == 0, jnp.stack([mine, got]), jnp.stack([got, mine]))
            rows = lax.all_gather(both.reshape(2 * local_rows, half), ("xl", "z"), axis=0, tiled=True)
        else:
            spread = jnp.broadcast_to(halves[None], (lanes // 2, 2, local_rows, half))
            rows = lax.all_to_all(spread.reshape(lanes, local_rows, half), ROW, 0, 0, tiled=True)
            rows = rows.reshape(lanes * local_rows, half)
        part = lax.dot_general(
            rows, up_all[layer_at], (((1,), (1,)), ((), ())), preferred_element_type=jnp.float32
        )
        pre_act = part + lax.ppermute(part, "c", SWAP)
        mask = jnp.repeat(live[layer_at], BLOCK)
        active = (jnp.maximum(pre_act, 0.0) * mask[None, :]).astype(jnp.bfloat16)
        out = jnp.dot(active, down_all[layer_at], preferred_element_type=jnp.float32)
        out = out.astype(jnp.bfloat16).reshape(lanes, local_rows, half)
        out = lax.all_to_all(out, ROW, 0, 0, tiled=True)
        total = jnp.sum(out.reshape(lanes // 2, 2, local_rows, half).astype(jnp.float32), axis=0)
        update = jnp.concatenate([total[0], total[1]], axis=1)
        residual = (residual.astype(jnp.float32) + update).astype(jnp.bfloat16)
    return residual


def solution(mesh):
    fine = Mesh(mesh.devices.reshape(2, 4, 2, 4, 2), ("xh", "y", "xl", "z", "c"))
    split = P(("xh", "y", "xl", "z", "c"), None)
    return jax.shard_map(
        body, mesh=fine, in_specs=(split, P(), split, split, P()), out_specs=split, check_vma=False
    )
```

```python
import jax
import jax.numpy as jnp
from jax import lax
from jax.experimental import pallas as pl
from jax.experimental.pallas import tpu as pltpu
from jax.sharding import Mesh
from jax.sharding import PartitionSpec as P

BLOCK = 128
LAYERS = 2
HELD = 6
ROW = ("xl", "z", "c")
SWAP = [(0, 1), (1, 0)]


def normalize(rows_in, gain_row):
    values = rows_in.astype(jnp.float32)
    row_mean = jnp.mean(values, axis=1, keepdims=True)
    centered = values - row_mean
    row_var = jnp.mean(centered * centered, axis=1, keepdims=True)
    return (centered * lax.rsqrt(row_var + 1e-05) * gain_row[None, :]).astype(jnp.bfloat16)


def pick_up(chosen, rows):
    groups, width = chosen.shape[0], rows.shape[1]

    def copy(chosen_ref, in_ref, out_ref):
        out_ref[0] = in_ref[...]

    return pl.pallas_call(
        copy,
        grid_spec=pltpu.PrefetchScalarGridSpec(
            num_scalar_prefetch=1,
            grid=(groups,),
            in_specs=[pl.BlockSpec((BLOCK, width), lambda g, ch: (ch[g], 0))],
            out_specs=pl.BlockSpec((1, BLOCK, width), lambda g, ch: (g, 0, 0)),
        ),
        out_shape=jax.ShapeDtypeStruct((groups, BLOCK, width), rows.dtype),
        compiler_params=pltpu.CompilerParams(vmem_limit_bytes=24 << 20),
        cost_estimate=pl.CostEstimate(flops=0, bytes_accessed=groups * BLOCK * width * 4, transcendentals=0),
        name="pick_up",
    )(chosen, rows)


def pick_down(table, rows, got):
    groups, half = (table.shape[0] - 1) // 2, got.shape[1]

    def copy(table_ref, own_ref, got_ref, out_ref):
        core = table_ref[2 * groups]
        out_ref[0, core] = own_ref[...]
        out_ref[0, 1 - core] = got_ref[...]

    return pl.pallas_call(
        copy,
        grid_spec=pltpu.PrefetchScalarGridSpec(
            num_scalar_prefetch=1,
            grid=(groups,),
            in_specs=[
                pl.BlockSpec((BLOCK, half), lambda g, tb: (tb[g], tb[2 * groups])),
                pl.BlockSpec((BLOCK, half), lambda g, tb: (tb[groups + g], 0)),
            ],
            out_specs=pl.BlockSpec((1, 2, BLOCK, half), lambda g, tb: (g, 0, 0, 0)),
        ),
        out_shape=jax.ShapeDtypeStruct((groups, 2, BLOCK, half), rows.dtype),
        compiler_params=pltpu.CompilerParams(vmem_limit_bytes=24 << 20),
        cost_estimate=pl.CostEstimate(flops=0, bytes_accessed=groups * BLOCK * half * 8, transcendentals=0),
        name="pick_down",
    )(table, rows, got)


def expand(core, layer_at, rows, up_own, up_got):
    slots = up_own.shape[0] // LAYERS
    count, half = rows.shape

    def kernel(core_ref, rows_ref, own_ref, got_ref, out_ref):
        def product(ref):
            return lax.dot_general(
                rows_ref[...], ref[0], (((1,), (1,)), ((), ())), preferred_element_type=jnp.float32
            )

        at = core_ref[0]
        out_ref[:, pl.ds(pl.multiple_of(at * BLOCK, BLOCK), BLOCK)] = product(own_ref)
        out_ref[:, pl.ds(pl.multiple_of((1 - at) * BLOCK, BLOCK), BLOCK)] = product(got_ref)

    return pl.pallas_call(
        kernel,
        grid_spec=pltpu.PrefetchScalarGridSpec(
            num_scalar_prefetch=1,
            grid=(slots,),
            in_specs=[
                pl.BlockSpec((count, half), lambda s, at: (0, 0)),
                pl.BlockSpec((1, BLOCK, half), lambda s, at: (layer_at * slots + s, 0, at[0])),
                pl.BlockSpec((1, BLOCK, half), lambda s, at: (layer_at * slots + s, 0, 0)),
            ],
            out_specs=pl.BlockSpec((count, 2 * BLOCK), lambda s, at: (0, s)),
        ),
        out_shape=jax.ShapeDtypeStruct((count, slots * 2 * BLOCK), jnp.float32),
        compiler_params=pltpu.CompilerParams(vmem_limit_bytes=24 << 20),
        cost_estimate=pl.CostEstimate(
            flops=4 * count * slots * BLOCK * half, bytes_accessed=slots * BLOCK * half * 4, transcendentals=0
        ),
        name="expand",
    )(core, rows, up_own, up_got)


def contract(layer_at, part, other, mask, down_all):
    slots, half = down_all.shape[0] // LAYERS, down_all.shape[3]
    count, hidden_units = part.shape
    tile = 512

    def kernel(part_ref, other_ref, mask_ref, down_ref, out_ref, active_ref):
        @pl.when(pl.program_id(0) == 0)
        def _():
            pre_act = part_ref[...] + other_ref[...]
            active_ref[...] = (jnp.maximum(pre_act, 0.0) * mask_ref[...]).astype(jnp.bfloat16)

        down = down_ref[...].reshape(hidden_units, tile)
        out_ref[...] = jnp.dot(active_ref[...], down, preferred_element_type=jnp.float32).astype(jnp.bfloat16)

    return pl.pallas_call(
        kernel,
        grid=(half // tile,),
        in_specs=[
            pl.BlockSpec((count, hidden_units), lambda n: (0, 0)),
            pl.BlockSpec((count, hidden_units), lambda n: (0, 0)),
            pl.BlockSpec((1, hidden_units), lambda n: (0, 0)),
            pl.BlockSpec((slots, 2, BLOCK, tile), lambda n: (layer_at, 0, 0, n)),
        ],
        out_specs=pl.BlockSpec((count, tile), lambda n: (0, n)),
        out_shape=jax.ShapeDtypeStruct((count, half), jnp.bfloat16),
        scratch_shapes=[pltpu.VMEM((count, hidden_units), jnp.bfloat16)],
        compiler_params=pltpu.CompilerParams(vmem_limit_bytes=24 << 20),
        cost_estimate=pl.CostEstimate(
            flops=2 * count * hidden_units * half, bytes_accessed=hidden_units * half * 2, transcendentals=0
        ),
        name="contract",
    )(part, other, mask, down_all)


def body(hidden, gains, up_rows, down_rows, pick):
    owners, lanes = 8, 16
    owner = lax.axis_index(("xh", "y"))
    chip_lane = lax.axis_index(("xl", "z")) * 2
    core = lax.axis_index("c")
    local_rows, width = hidden.shape
    half = width // 2
    sent = jnp.minimum(lax.dynamic_slice_in_dim(pick, owner * lanes + chip_lane, 2, 1), HELD - 1)
    own_sent = lax.dynamic_index_in_dim(sent, core, 1, keepdims=False)
    other_sent = lax.dynamic_index_in_dim(sent, 1 - core, 1, keepdims=False)
    group_picks = lax.dynamic_slice_in_dim(pick, owner, 1, 0).reshape(owners, lanes)
    pair_picks = lax.dynamic_slice_in_dim(group_picks, chip_lane, 2, 1)
    live = (pair_picks < HELD).astype(jnp.float32).reshape(LAYERS, owners // LAYERS * 2)
    core_at = core.reshape(1)

    def other_half(array):
        return lax.dynamic_slice_in_dim(array, (1 - core) * half, half, array.ndim - 1)

    up_own = lax.all_to_all(pick_up(own_sent, up_rows), ("xh", "y"), 0, 0, tiled=True)
    down_got = lax.ppermute(other_half(down_rows), "c", SWAP)
    table = jnp.concatenate([own_sent, other_sent, core_at])
    down_all = lax.all_to_all(pick_down(table, down_rows, down_got), ("xh", "y"), 0, 0, tiled=True)
    up_got = lax.ppermute(other_half(up_own), "c", SWAP)

    residual = hidden
    for layer_at in range(LAYERS):
        normed = normalize(residual, gains[layer_at])
        if layer_at == 0:
            mine = lax.dynamic_slice_in_dim(normed, core * half, half, 1)
            got = lax.ppermute(other_half(normed), "c", SWAP)
            both = jnp.where(core == 0, jnp.stack([mine, got]), jnp.stack([got, mine]))
            rows = lax.all_gather(both.reshape(2 * local_rows, half), ("xl", "z"), axis=0, tiled=True)
        else:
            halves = jnp.stack([normed[:, :half], normed[:, half:]])
            spread = jnp.broadcast_to(halves[None], (lanes // 2, 2, local_rows, half))
            rows = lax.all_to_all(spread.reshape(lanes, local_rows, half), ROW, 0, 0, tiled=True)
            rows = rows.reshape(lanes * local_rows, half)
        part = expand(core_at, layer_at, rows, up_own, up_got)
        mask = jnp.repeat(live[layer_at], BLOCK)[None, :]
        out = contract(layer_at, part, lax.ppermute(part, "c", SWAP), mask, down_all)
        out = lax.all_to_all(out.reshape(lanes, local_rows, half), ROW, 0, 0, tiled=True)
        total = jnp.sum(out.reshape(lanes // 2, 2, local_rows, half).astype(jnp.float32), axis=0)
        update = jnp.concatenate([total[0], total[1]], axis=1)
        residual = (residual.astype(jnp.float32) + update).astype(jnp.bfloat16)
    return residual


def solution(mesh):
    fine = Mesh(mesh.devices.reshape(2, 4, 2, 4, 2), ("xh", "y", "xl", "z", "c"))
    split = P(("xh", "y", "xl", "z", "c"), None)
    return jax.shard_map(
        body, mesh=fine, in_specs=(split, P(), split, split, P()), out_specs=split, check_vma=False
    )
```

```python
import jax
import jax.numpy as jnp
from jax import lax
from jax.experimental import pallas as pl
from jax.experimental.pallas import tpu as pltpu
from jax.sharding import Mesh
from jax.sharding import PartitionSpec as P

BLOCK = 128
LAYERS = 2
HELD = 6
ALL = ("xh", "y", "xl", "z", "c")
ROW = ("xl", "z", "c")
SWAP = [(0, 1), (1, 0)]


def normalize(rows_in, gain_row):
    values = rows_in.astype(jnp.float32)
    row_mean = jnp.mean(values, axis=1, keepdims=True)
    centered = values - row_mean
    row_var = jnp.mean(centered * centered, axis=1, keepdims=True)
    return (centered * lax.rsqrt(row_var + 1e-05) * gain_row[None, :]).astype(jnp.bfloat16)


def pick_up(chosen, rows):
    groups, width = chosen.shape[0], rows.shape[1]

    def copy(chosen_ref, in_ref, out_ref):
        out_ref[0] = in_ref[...]

    return pl.pallas_call(
        copy,
        grid_spec=pltpu.PrefetchScalarGridSpec(
            num_scalar_prefetch=1,
            grid=(groups,),
            in_specs=[pl.BlockSpec((BLOCK, width), lambda g, ch: (ch[g], 0))],
            out_specs=pl.BlockSpec((1, BLOCK, width), lambda g, ch: (g, 0, 0)),
        ),
        out_shape=jax.ShapeDtypeStruct((groups, BLOCK, width), rows.dtype),
        compiler_params=pltpu.CompilerParams(vmem_limit_bytes=24 << 20),
        cost_estimate=pl.CostEstimate(flops=0, bytes_accessed=groups * BLOCK * width * 4, transcendentals=0),
        name="pick_up",
    )(chosen, rows)


def pick_down(table, rows, got):
    groups, half = (table.shape[0] - 1) // 2, got.shape[1]

    def copy(table_ref, own_ref, got_ref, out_ref):
        core = table_ref[2 * groups]
        out_ref[0, core] = own_ref[...]
        out_ref[0, 1 - core] = got_ref[...]

    return pl.pallas_call(
        copy,
        grid_spec=pltpu.PrefetchScalarGridSpec(
            num_scalar_prefetch=1,
            grid=(groups,),
            in_specs=[
                pl.BlockSpec((BLOCK, half), lambda g, tb: (tb[g], tb[2 * groups])),
                pl.BlockSpec((BLOCK, half), lambda g, tb: (tb[groups + g], 0)),
            ],
            out_specs=pl.BlockSpec((1, 2, BLOCK, half), lambda g, tb: (g, 0, 0, 0)),
        ),
        out_shape=jax.ShapeDtypeStruct((groups, 2, BLOCK, half), rows.dtype),
        compiler_params=pltpu.CompilerParams(vmem_limit_bytes=24 << 20),
        cost_estimate=pl.CostEstimate(flops=0, bytes_accessed=groups * BLOCK * half * 8, transcendentals=0),
        name="pick_down",
    )(table, rows, got)


def expand(core, layer_at, rows, up_own, up_got):
    slots = up_own.shape[0] // LAYERS
    count, half = rows.shape
    step = 2
    wide = step * BLOCK

    def kernel(core_ref, rows_ref, own_ref, got_ref, out_ref):
        def product(ref):
            return lax.dot_general(
                rows_ref[...],
                ref[...].reshape(wide, half),
                (((1,), (1,)), ((), ())),
                preferred_element_type=jnp.float32,
            )

        at, done = core_ref[0], pl.program_id(0) * wide
        out_ref[:, pl.ds(pl.multiple_of(at * slots * BLOCK + done, wide), wide)] = product(own_ref)
        out_ref[:, pl.ds(pl.multiple_of((1 - at) * slots * BLOCK + done, wide), wide)] = product(got_ref)

    first = layer_at * slots // step
    return pl.pallas_call(
        kernel,
        grid_spec=pltpu.PrefetchScalarGridSpec(
            num_scalar_prefetch=1,
            grid=(slots // step,),
            in_specs=[
                pl.BlockSpec((count, half), lambda s, at: (0, 0)),
                pl.BlockSpec((step, BLOCK, half), lambda s, at: (first + s, 0, at[0])),
                pl.BlockSpec((step, BLOCK, half), lambda s, at: (first + s, 0, 0)),
            ],
            out_specs=pl.BlockSpec((count, slots * 2 * BLOCK), lambda s, at: (0, 0)),
        ),
        out_shape=jax.ShapeDtypeStruct((count, slots * 2 * BLOCK), jnp.float32),
        compiler_params=pltpu.CompilerParams(vmem_limit_bytes=32 << 20),
        cost_estimate=pl.CostEstimate(
            flops=4 * count * slots * BLOCK * half, bytes_accessed=slots * BLOCK * half * 4, transcendentals=0
        ),
        name="expand",
    )(core, rows, up_own, up_got)


def contract(layer_at, part, other, mask, down_all):
    slots, half = down_all.shape[0] // LAYERS, down_all.shape[3]
    count, hidden_units = part.shape
    per_unit = hidden_units // 2
    tile = 1024

    def kernel(part_ref, other_ref, mask_ref, down_ref, out_ref, active_ref):
        @pl.when(pl.program_id(0) == 0)
        def _():
            pre_act = part_ref[...] + other_ref[...]
            active_ref[...] = (jnp.maximum(pre_act, 0.0) * mask_ref[...]).astype(jnp.bfloat16)

        total = jnp.dot(
            active_ref[:, :per_unit], down_ref[:, 0].reshape(per_unit, tile), preferred_element_type=jnp.float32
        )
        total += jnp.dot(
            active_ref[:, per_unit:], down_ref[:, 1].reshape(per_unit, tile), preferred_element_type=jnp.float32
        )
        out_ref[...] = total.astype(jnp.bfloat16)

    return pl.pallas_call(
        kernel,
        grid=(half // tile,),
        in_specs=[
            pl.BlockSpec((count, hidden_units), lambda n: (0, 0)),
            pl.BlockSpec((count, hidden_units), lambda n: (0, 0)),
            pl.BlockSpec((1, hidden_units), lambda n: (0, 0)),
            pl.BlockSpec((slots, 2, BLOCK, tile), lambda n: (layer_at, 0, 0, n)),
        ],
        out_specs=pl.BlockSpec((count, tile), lambda n: (0, n)),
        out_shape=jax.ShapeDtypeStruct((count, half), jnp.bfloat16),
        scratch_shapes=[pltpu.VMEM((count, hidden_units), jnp.bfloat16)],
        compiler_params=pltpu.CompilerParams(vmem_limit_bytes=32 << 20),
        cost_estimate=pl.CostEstimate(
            flops=2 * count * hidden_units * half, bytes_accessed=hidden_units * half * 2, transcendentals=0
        ),
        name="contract",
    )(part, other, mask, down_all)


def device(x, y, z, c):
    return (((x // 2 * 4 + y) * 2 + x % 2) * 4 + z) * 2 + c


def to_groups(blocks):
    sets = [
        [device(x, y, z, c) for x in pair for y in range(4)]
        for pair in ((0, 3), (1, 2))
        for z in range(4)
        for c in range(2)
    ]
    return lax.all_to_all(blocks, ALL, 0, 0, tiled=True, axis_index_groups=sets)


def body(hidden, gains, up_rows, down_rows, pick):
    owners, lanes = 8, 16
    owner = lax.axis_index(("xh", "y"))
    chip_lane = lax.axis_index(("xl", "z")) * 2
    core = lax.axis_index("c")
    local_rows, width = hidden.shape
    half = width // 2
    sent = jnp.minimum(lax.dynamic_slice_in_dim(pick, owner * lanes + chip_lane, 2, 1), HELD - 1)
    own_sent = lax.dynamic_index_in_dim(sent, core, 1, keepdims=False)
    other_sent = lax.dynamic_index_in_dim(sent, 1 - core, 1, keepdims=False)
    group_picks = lax.dynamic_slice_in_dim(pick, owner, 1, 0).reshape(LAYERS, owners // LAYERS, 2, 4, 2)
    side = lax.axis_index("xl") ^ lax.axis_index("xh")
    masks = []
    for layer_at in range(LAYERS):
        lane_picks = lax.dynamic_index_in_dim(group_picks[layer_at], side ^ layer_at, 1, keepdims=False)
        lane_picks = lax.dynamic_index_in_dim(lane_picks, lax.axis_index("z"), 1, keepdims=False)
        live = (lane_picks < HELD).astype(jnp.float32).T.reshape(-1)
        masks.append(jnp.repeat(live, BLOCK)[None, :])
    core_at = core.reshape(1)

    def other_half(array):
        return lax.dynamic_slice_in_dim(array, (1 - core) * half, half, array.ndim - 1)

    up_own = to_groups(pick_up(own_sent, up_rows))
    down_got = lax.ppermute(other_half(down_rows), "c", SWAP)
    table = jnp.concatenate([own_sent, other_sent, core_at])
    down_all = to_groups(pick_down(table, down_rows, down_got))
    up_got = lax.ppermute(other_half(up_own), "c", SWAP)

    residual = hidden
    for layer_at in range(LAYERS):
        normed = normalize(residual, gains[layer_at])
        if layer_at == 0:
            mine = lax.dynamic_slice_in_dim(normed, core * half, half, 1)
            got = lax.ppermute(other_half(normed), "c", SWAP)
            both = jnp.where(core == 0, jnp.stack([mine, got]), jnp.stack([got, mine]))
            rows = lax.all_gather(both.reshape(2 * local_rows, half), ("xl", "z"), axis=0, tiled=True)
        else:
            halves = jnp.stack([normed[:, :half], normed[:, half:]])
            spread = jnp.broadcast_to(halves[None], (lanes // 2, 2, local_rows, half))
            rows = lax.all_to_all(spread.reshape(lanes, local_rows, half), ROW, 0, 0, tiled=True)
            rows = rows.reshape(lanes * local_rows, half)
        part = expand(core_at, layer_at, rows, up_own, up_got)
        out = contract(layer_at, part, lax.ppermute(part, "c", SWAP), masks[layer_at], down_all)
        out = lax.all_to_all(out.reshape(lanes, local_rows, half), ROW, 0, 0, tiled=True)
        total = jnp.sum(out.reshape(lanes // 2, 2, local_rows, half).astype(jnp.float32), axis=0)
        update = jnp.concatenate([total[0], total[1]], axis=1)
        residual = (residual.astype(jnp.float32) + update).astype(jnp.bfloat16)
    return residual


def solution(mesh):
    fine = Mesh(mesh.devices.reshape(2, 4, 2, 4, 2), ALL)
    split = P(ALL, None)
    return jax.shard_map(
        body, mesh=fine, in_specs=(split, P(), split, split, P()), out_specs=split, check_vma=False
    )
```

```python
import jax
import jax.numpy as jnp
from jax import lax
from jax.experimental import pallas as pl
from jax.experimental.pallas import tpu as pltpu
from jax.sharding import Mesh
from jax.sharding import PartitionSpec as P

BLOCK = 128
LAYERS = 2
HELD = 6
TILE = 1024
ALL = ("xh", "y", "xl", "z", "c")
ROW = ("xl", "z", "c")
SWAP = [(0, 1), (1, 0)]


def normalize(rows_in, gain_row):
    values = rows_in.astype(jnp.float32)
    row_mean = jnp.mean(values, axis=1, keepdims=True)
    centered = values - row_mean
    row_var = jnp.mean(centered * centered, axis=1, keepdims=True)
    return (centered * lax.rsqrt(row_var + 1e-05) * gain_row[None, :]).astype(jnp.bfloat16)


def pick_up(chosen, rows):
    groups, width = chosen.shape[0], rows.shape[1]

    def copy(chosen_ref, in_ref, out_ref):
        out_ref[0] = in_ref[...]

    return pl.pallas_call(
        copy,
        grid_spec=pltpu.PrefetchScalarGridSpec(
            num_scalar_prefetch=1,
            grid=(groups,),
            in_specs=[pl.BlockSpec((BLOCK, width), lambda g, ch: (ch[g], 0))],
            out_specs=pl.BlockSpec((1, BLOCK, width), lambda g, ch: (g, 0, 0)),
        ),
        out_shape=jax.ShapeDtypeStruct((groups, BLOCK, width), rows.dtype),
        compiler_params=pltpu.CompilerParams(vmem_limit_bytes=24 << 20),
        cost_estimate=pl.CostEstimate(flops=0, bytes_accessed=groups * BLOCK * width * 4, transcendentals=0),
        name="pick_up",
    )(chosen, rows)


def pick_down(table, rows, got, first, count):
    groups, tiles = (table.shape[0] - 1) // 2, got.shape[1] // TILE

    def copy(table_ref, own_ref, got_ref, out_ref):
        core = table_ref[2 * groups]
        out_ref[0, core] = own_ref[...]
        out_ref[0, 1 - core] = got_ref[...]

    return pl.pallas_call(
        copy,
        grid_spec=pltpu.PrefetchScalarGridSpec(
            num_scalar_prefetch=1,
            grid=(groups, count),
            in_specs=[
                pl.BlockSpec((BLOCK, TILE), lambda g, n, tb: (tb[g], tb[2 * groups] * tiles + first + n)),
                pl.BlockSpec((BLOCK, TILE), lambda g, n, tb: (tb[groups + g], first + n)),
            ],
            out_specs=pl.BlockSpec((1, 2, BLOCK, TILE), lambda g, n, tb: (g, 0, 0, n)),
        ),
        out_shape=jax.ShapeDtypeStruct((groups, 2, BLOCK, count * TILE), rows.dtype),
        compiler_params=pltpu.CompilerParams(vmem_limit_bytes=24 << 20),
        cost_estimate=pl.CostEstimate(flops=0, bytes_accessed=groups * BLOCK * count * TILE * 8, transcendentals=0),
        name="pick_down",
    )(table, rows, got)


def expand(core, layer_at, rows, up_own, up_got):
    slots = up_own.shape[0] // LAYERS
    count, half = rows.shape
    step = 2
    wide = step * BLOCK

    def kernel(core_ref, rows_ref, own_ref, got_ref, out_ref):
        def product(ref):
            return lax.dot_general(
                rows_ref[...],
                ref[...].reshape(wide, half),
                (((1,), (1,)), ((), ())),
                preferred_element_type=jnp.float32,
            )

        at, done = core_ref[0], pl.program_id(0) * wide
        out_ref[:, pl.ds(pl.multiple_of(at * slots * BLOCK + done, wide), wide)] = product(own_ref)
        out_ref[:, pl.ds(pl.multiple_of((1 - at) * slots * BLOCK + done, wide), wide)] = product(got_ref)

    first = layer_at * slots // step
    return pl.pallas_call(
        kernel,
        grid_spec=pltpu.PrefetchScalarGridSpec(
            num_scalar_prefetch=1,
            grid=(slots // step,),
            in_specs=[
                pl.BlockSpec((count, half), lambda s, at: (0, 0)),
                pl.BlockSpec((step, BLOCK, half), lambda s, at: (first + s, 0, at[0])),
                pl.BlockSpec((step, BLOCK, half), lambda s, at: (first + s, 0, 0)),
            ],
            out_specs=pl.BlockSpec((count, slots * 2 * BLOCK), lambda s, at: (0, 0)),
        ),
        out_shape=jax.ShapeDtypeStruct((count, slots * 2 * BLOCK), jnp.float32),
        compiler_params=pltpu.CompilerParams(vmem_limit_bytes=32 << 20),
        cost_estimate=pl.CostEstimate(
            flops=4 * count * slots * BLOCK * half, bytes_accessed=slots * BLOCK * half * 4, transcendentals=0
        ),
        name="expand",
    )(core, rows, up_own, up_got)


def contract(layer_at, part, other, mask, *parts):
    slots = parts[0].shape[0] // LAYERS
    count, hidden_units = part.shape
    per_unit = hidden_units // 2
    tiles = [array.shape[3] // TILE for array in parts]
    starts = [sum(tiles[:i]) for i in range(len(tiles))]

    def kernel(part_ref, other_ref, mask_ref, *refs):
        down_refs, out_ref, active_ref = refs[: len(parts)], refs[-2], refs[-1]
        at = pl.program_id(0)

        @pl.when(at == 0)
        def _():
            pre_act = part_ref[...] + other_ref[...]
            active_ref[...] = (jnp.maximum(pre_act, 0.0) * mask_ref[...]).astype(jnp.bfloat16)

        for ref, start, number in zip(down_refs, starts, tiles):

            @pl.when((at >= start) & (at < start + number))
            def _(ref=ref):
                total = jnp.dot(
                    active_ref[:, :per_unit], ref[:, 0].reshape(per_unit, TILE), preferred_element_type=jnp.float32
                )
                total += jnp.dot(
                    active_ref[:, per_unit:], ref[:, 1].reshape(per_unit, TILE), preferred_element_type=jnp.float32
                )
                out_ref[...] = total.astype(jnp.bfloat16)

    def down_spec(start, number):
        return pl.BlockSpec(
            (slots, 2, BLOCK, TILE), lambda n: (layer_at, 0, 0, jnp.clip(n - start, 0, number - 1))
        )

    return pl.pallas_call(
        kernel,
        grid=(sum(tiles),),
        in_specs=[
            pl.BlockSpec((count, hidden_units), lambda n: (0, 0)),
            pl.BlockSpec((count, hidden_units), lambda n: (0, 0)),
            pl.BlockSpec((1, hidden_units), lambda n: (0, 0)),
            *[down_spec(start, number) for start, number in zip(starts, tiles)],
        ],
        out_specs=pl.BlockSpec((count, TILE), lambda n: (0, n)),
        out_shape=jax.ShapeDtypeStruct((count, sum(tiles) * TILE), jnp.bfloat16),
        scratch_shapes=[pltpu.VMEM((count, hidden_units), jnp.bfloat16)],
        compiler_params=pltpu.CompilerParams(vmem_limit_bytes=32 << 20),
        cost_estimate=pl.CostEstimate(
            flops=2 * count * hidden_units * sum(tiles) * TILE,
            bytes_accessed=hidden_units * sum(tiles) * TILE * 2,
            transcendentals=0,
        ),
        name="contract",
    )(part, other, mask, *parts)


def sum_lanes(out):
    lanes, local_rows = 16, out.shape[0] // 16
    out = lax.all_to_all(out.reshape(lanes, local_rows, out.shape[1]), ROW, 0, 0, tiled=True)
    return jnp.sum(out.reshape(lanes // 2, 2, local_rows, -1).astype(jnp.float32), axis=0)


def in_order(core, mine, got):
    return jnp.where(core == 0, jnp.stack([mine, got]), jnp.stack([got, mine]))


def device(x, y, z, c):
    return (((x // 2 * 4 + y) * 2 + x % 2) * 4 + z) * 2 + c


def to_groups(blocks):
    sets = [
        [device(x, y, z, c) for x in pair for y in range(4)]
        for pair in ((0, 3), (1, 2))
        for z in range(4)
        for c in range(2)
    ]
    return lax.all_to_all(blocks, ALL, 0, 0, tiled=True, axis_index_groups=sets)


def body(hidden, gains, up_rows, down_rows, pick):
    owners, lanes = 8, 16
    owner = lax.axis_index(("xh", "y"))
    chip_lane = lax.axis_index(("xl", "z")) * 2
    core = lax.axis_index("c")
    local_rows, width = hidden.shape
    half = width // 2
    sent = jnp.minimum(lax.dynamic_slice_in_dim(pick, owner * lanes + chip_lane, 2, 1), HELD - 1)
    own_sent = lax.dynamic_index_in_dim(sent, core, 1, keepdims=False)
    other_sent = lax.dynamic_index_in_dim(sent, 1 - core, 1, keepdims=False)
    group_picks = lax.dynamic_slice_in_dim(pick, owner, 1, 0).reshape(LAYERS, owners // LAYERS, 2, 4, 2)
    side = lax.axis_index("xl") ^ lax.axis_index("xh")
    masks = []
    for layer_at in range(LAYERS):
        lane_picks = lax.dynamic_index_in_dim(group_picks[layer_at], side ^ layer_at, 1, keepdims=False)
        lane_picks = lax.dynamic_index_in_dim(lane_picks, lax.axis_index("z"), 1, keepdims=False)
        live = (lane_picks < HELD).astype(jnp.float32).T.reshape(-1)
        masks.append(jnp.repeat(live, BLOCK)[None, :])
    core_at = core.reshape(1)

    def other_half(array):
        return lax.dynamic_slice_in_dim(array, (1 - core) * half, half, array.ndim - 1)

    up_own = to_groups(pick_up(own_sent, up_rows))
    down_got = lax.ppermute(other_half(down_rows), "c", SWAP)
    table = jnp.concatenate([own_sent, other_sent, core_at])
    tiles = half // TILE
    early = to_groups(pick_down(table, down_rows, down_got, 0, tiles - 1))
    late = to_groups(pick_down(table, down_rows, down_got, tiles - 1, 1))
    up_got = lax.ppermute(other_half(up_own), "c", SWAP)

    residual = hidden
    for layer_at in range(LAYERS):
        normed = normalize(residual, gains[layer_at])
        if layer_at == 0:
            mine = lax.dynamic_slice_in_dim(normed, core * half, half, 1)
            got = lax.ppermute(other_half(normed), "c", SWAP)
            rows = lax.all_gather(in_order(core, mine, got).reshape(2 * local_rows, half), ("xl", "z"), axis=0, tiled=True)
        else:
            halves = jnp.stack([normed[:, :half], normed[:, half:]])
            spread = jnp.broadcast_to(halves[None], (lanes // 2, 2, local_rows, half))
            rows = lax.all_to_all(spread.reshape(lanes, local_rows, half), ROW, 0, 0, tiled=True)
            rows = rows.reshape(lanes * local_rows, half)
        part = expand(core_at, layer_at, rows, up_own, up_got)
        other = lax.ppermute(part, "c", SWAP)
        if layer_at == 0:
            first = contract(layer_at, part, other, masks[layer_at], early)
            first = lax.psum_scatter(first, ("xl", "z"), scatter_dimension=0, tiled=True)
            mine = lax.dynamic_slice_in_dim(first, core * local_rows, local_rows, 0)
            got = lax.dynamic_slice_in_dim(first, (1 - core) * local_rows, local_rows, 0)
            first = in_order(core, mine, lax.ppermute(got, "c", SWAP)).astype(jnp.float32)
            second = sum_lanes(contract(layer_at, part, other, masks[layer_at], late))
            total = jnp.concatenate([first, second], axis=2)
        else:
            total = sum_lanes(contract(layer_at, part, other, masks[layer_at], early, late))
        update = jnp.concatenate([total[0], total[1]], axis=1)
        residual = (residual.astype(jnp.float32) + update).astype(jnp.bfloat16)
    return residual


def solution(mesh):
    fine = Mesh(mesh.devices.reshape(2, 4, 2, 4, 2), ALL)
    split = P(ALL, None)
    return jax.shard_map(
        body, mesh=fine, in_specs=(split, P(), split, split, P()), out_specs=split, check_vma=False
    )
```

```python
import jax
import jax.numpy as jnp
from jax import lax
from jax.experimental import pallas as pl
from jax.experimental.pallas import tpu as pltpu
from jax.sharding import Mesh
from jax.sharding import PartitionSpec as P

BLOCK = 128
LAYERS = 2
HELD = 6
TILE = 1024
ALL = ("xh", "y", "xl", "z", "c")
ROW = ("xl", "z", "c")
SWAP = [(0, 1), (1, 0)]


def normalize(rows_in, gain_row):
    values = rows_in.astype(jnp.float32)
    row_mean = jnp.mean(values, axis=1, keepdims=True)
    centered = values - row_mean
    row_var = jnp.mean(centered * centered, axis=1, keepdims=True)
    return (centered * lax.rsqrt(row_var + 1e-05) * gain_row[None, :]).astype(jnp.bfloat16)


def pick_up(chosen, rows):
    groups, width = chosen.shape[0], rows.shape[1]

    def copy(chosen_ref, in_ref, out_ref):
        out_ref[0] = in_ref[...]

    return pl.pallas_call(
        copy,
        grid_spec=pltpu.PrefetchScalarGridSpec(
            num_scalar_prefetch=1,
            grid=(groups,),
            in_specs=[pl.BlockSpec((BLOCK, width), lambda g, ch: (ch[g], 0))],
            out_specs=pl.BlockSpec((1, BLOCK, width), lambda g, ch: (g, 0, 0)),
        ),
        out_shape=jax.ShapeDtypeStruct((groups, BLOCK, width), rows.dtype),
        compiler_params=pltpu.CompilerParams(vmem_limit_bytes=24 << 20),
        cost_estimate=pl.CostEstimate(flops=0, bytes_accessed=groups * BLOCK * width * 4, transcendentals=0),
        name="pick_up",
    )(chosen, rows)


def pick_down(table, rows, got, first, count):
    groups, tiles = (table.shape[0] - 1) // 2, got.shape[1] // TILE

    def copy(table_ref, own_ref, got_ref, out_ref):
        core = table_ref[2 * groups]
        out_ref[0, core] = own_ref[...]
        out_ref[0, 1 - core] = got_ref[...]

    return pl.pallas_call(
        copy,
        grid_spec=pltpu.PrefetchScalarGridSpec(
            num_scalar_prefetch=1,
            grid=(groups, count),
            in_specs=[
                pl.BlockSpec((BLOCK, TILE), lambda g, n, tb: (tb[g], tb[2 * groups] * tiles + first + n)),
                pl.BlockSpec((BLOCK, TILE), lambda g, n, tb: (tb[groups + g], first + n)),
            ],
            out_specs=pl.BlockSpec((1, 2, BLOCK, TILE), lambda g, n, tb: (g, 0, 0, n)),
        ),
        out_shape=jax.ShapeDtypeStruct((groups, 2, BLOCK, count * TILE), rows.dtype),
        compiler_params=pltpu.CompilerParams(vmem_limit_bytes=24 << 20),
        cost_estimate=pl.CostEstimate(flops=0, bytes_accessed=groups * BLOCK * count * TILE * 8, transcendentals=0),
        name="pick_down",
    )(table, rows, got)


def expand(core, layer_at, rows, up_own, up_got):
    slots = up_own.shape[0] // LAYERS
    count, half = rows.shape
    step = 2
    wide = step * BLOCK

    def kernel(core_ref, rows_ref, own_ref, got_ref, out_ref, send_ref):
        def product(ref):
            return lax.dot_general(
                rows_ref[...],
                ref[...].reshape(wide, half),
                (((1,), (1,)), ((), ())),
                preferred_element_type=jnp.float32,
            )

        at, done = core_ref[0], pl.program_id(0) * wide
        for unit, ref in ((at, own_ref), (1 - at, got_ref)):
            columns = pl.ds(pl.multiple_of(unit * slots * BLOCK + done, wide), wide)
            share = product(ref)
            out_ref[:, columns] = share
            send_ref[:, columns] = share.astype(jnp.bfloat16)

    first = layer_at * slots // step
    return pl.pallas_call(
        kernel,
        grid_spec=pltpu.PrefetchScalarGridSpec(
            num_scalar_prefetch=1,
            grid=(slots // step,),
            in_specs=[
                pl.BlockSpec((count, half), lambda s, at: (0, 0)),
                pl.BlockSpec((step, BLOCK, half), lambda s, at: (first + s, 0, at[0])),
                pl.BlockSpec((step, BLOCK, half), lambda s, at: (first + s, 0, 0)),
            ],
            out_specs=[pl.BlockSpec((count, slots * 2 * BLOCK), lambda s, at: (0, 0))] * 2,
        ),
        out_shape=[jax.ShapeDtypeStruct((count, slots * 2 * BLOCK), t) for t in (jnp.float32, jnp.bfloat16)],
        compiler_params=pltpu.CompilerParams(vmem_limit_bytes=32 << 20),
        cost_estimate=pl.CostEstimate(
            flops=4 * count * slots * BLOCK * half, bytes_accessed=slots * BLOCK * half * 4, transcendentals=0
        ),
        name="expand",
    )(core, rows, up_own, up_got)


def contract(layer_at, part, other, mask, *parts):
    slots = parts[0].shape[0] // LAYERS
    count, hidden_units = part.shape
    per_unit = hidden_units // 2
    tiles = [array.shape[3] // TILE for array in parts]
    starts = [sum(tiles[:i]) for i in range(len(tiles))]

    def kernel(part_ref, other_ref, mask_ref, *refs):
        down_refs, out_ref, active_ref = refs[: len(parts)], refs[-2], refs[-1]
        at = pl.program_id(0)

        @pl.when(at == 0)
        def _():
            pre_act = part_ref[...] + other_ref[...].astype(jnp.float32)
            active_ref[...] = (jnp.maximum(pre_act, 0.0) * mask_ref[...]).astype(jnp.bfloat16)

        for ref, start, number in zip(down_refs, starts, tiles):

            @pl.when((at >= start) & (at < start + number))
            def _(ref=ref):
                total = jnp.dot(
                    active_ref[:, :per_unit], ref[:, 0].reshape(per_unit, TILE), preferred_element_type=jnp.float32
                )
                total += jnp.dot(
                    active_ref[:, per_unit:], ref[:, 1].reshape(per_unit, TILE), preferred_element_type=jnp.float32
                )
                out_ref[...] = total.astype(jnp.bfloat16)

    def down_spec(start, number):
        return pl.BlockSpec(
            (slots, 2, BLOCK, TILE), lambda n: (layer_at, 0, 0, jnp.clip(n - start, 0, number - 1))
        )

    return pl.pallas_call(
        kernel,
        grid=(sum(tiles),),
        in_specs=[
            pl.BlockSpec((count, hidden_units), lambda n: (0, 0)),
            pl.BlockSpec((count, hidden_units), lambda n: (0, 0)),
            pl.BlockSpec((1, hidden_units), lambda n: (0, 0)),
            *[down_spec(start, number) for start, number in zip(starts, tiles)],
        ],
        out_specs=pl.BlockSpec((count, TILE), lambda n: (0, n)),
        out_shape=jax.ShapeDtypeStruct((count, sum(tiles) * TILE), jnp.bfloat16),
        scratch_shapes=[pltpu.VMEM((count, hidden_units), jnp.bfloat16)],
        compiler_params=pltpu.CompilerParams(vmem_limit_bytes=32 << 20),
        cost_estimate=pl.CostEstimate(
            flops=2 * count * hidden_units * sum(tiles) * TILE,
            bytes_accessed=hidden_units * sum(tiles) * TILE * 2,
            transcendentals=0,
        ),
        name="contract",
    )(part, other, mask, *parts)


def sum_lanes(out):
    lanes, local_rows = 16, out.shape[0] // 16
    out = lax.all_to_all(out.reshape(lanes, local_rows, out.shape[1]), ROW, 0, 0, tiled=True)
    return jnp.sum(out.reshape(lanes // 2, 2, local_rows, -1).astype(jnp.float32), axis=0)


def in_order(core, mine, got):
    return jnp.where(core == 0, jnp.stack([mine, got]), jnp.stack([got, mine]))


def device(x, y, z, c):
    return (((x // 2 * 4 + y) * 2 + x % 2) * 4 + z) * 2 + c


def to_groups(blocks):
    sets = [
        [device(x, y, z, c) for x in pair for y in range(4)]
        for pair in ((0, 3), (1, 2))
        for z in range(4)
        for c in range(2)
    ]
    return lax.all_to_all(blocks, ALL, 0, 0, tiled=True, axis_index_groups=sets)


def body(hidden, gains, up_rows, down_rows, pick):
    owners, lanes = 8, 16
    owner = lax.axis_index(("xh", "y"))
    chip_lane = lax.axis_index(("xl", "z")) * 2
    core = lax.axis_index("c")
    local_rows, width = hidden.shape
    half = width // 2
    sent = jnp.minimum(lax.dynamic_slice_in_dim(pick, owner * lanes + chip_lane, 2, 1), HELD - 1)
    own_sent = lax.dynamic_index_in_dim(sent, core, 1, keepdims=False)
    other_sent = lax.dynamic_index_in_dim(sent, 1 - core, 1, keepdims=False)
    group_picks = lax.dynamic_slice_in_dim(pick, owner, 1, 0).reshape(LAYERS, owners // LAYERS, 2, 4, 2)
    side = lax.axis_index("xl") ^ lax.axis_index("xh")
    masks = []
    for layer_at in range(LAYERS):
        lane_picks = lax.dynamic_index_in_dim(group_picks[layer_at], side ^ layer_at, 1, keepdims=False)
        lane_picks = lax.dynamic_index_in_dim(lane_picks, lax.axis_index("z"), 1, keepdims=False)
        live = (lane_picks < HELD).astype(jnp.float32).T.reshape(-1)
        masks.append(jnp.repeat(live, BLOCK)[None, :])
    core_at = core.reshape(1)

    def other_half(array):
        return lax.dynamic_slice_in_dim(array, (1 - core) * half, half, array.ndim - 1)

    up_own = to_groups(pick_up(own_sent, up_rows))
    down_got = lax.ppermute(other_half(down_rows), "c", SWAP)
    table = jnp.concatenate([own_sent, other_sent, core_at])
    tiles = half // TILE
    early = to_groups(pick_down(table, down_rows, down_got, 0, tiles - 1))
    late = to_groups(pick_down(table, down_rows, down_got, tiles - 1, 1))
    up_got = lax.ppermute(other_half(up_own), "c", SWAP)

    residual = hidden
    for layer_at in range(LAYERS):
        normed = normalize(residual, gains[layer_at])
        if layer_at == 0:
            mine = lax.dynamic_slice_in_dim(normed, core * half, half, 1)
            got = lax.ppermute(other_half(normed), "c", SWAP)
            rows = lax.all_gather(in_order(core, mine, got).reshape(2 * local_rows, half), ("xl", "z"), axis=0, tiled=True)
        else:
            halves = jnp.stack([normed[:, :half], normed[:, half:]])
            spread = jnp.broadcast_to(halves[None], (lanes // 2, 2, local_rows, half))
            rows = lax.all_to_all(spread.reshape(lanes, local_rows, half), ROW, 0, 0, tiled=True)
            rows = rows.reshape(lanes * local_rows, half)
        part, sent_part = expand(core_at, layer_at, rows, up_own, up_got)
        other = lax.ppermute(sent_part, "c", SWAP)
        if layer_at == 0:
            first = contract(layer_at, part, other, masks[layer_at], early)
            first = lax.psum_scatter(first, ("xl", "z"), scatter_dimension=0, tiled=True)
            mine = lax.dynamic_slice_in_dim(first, core * local_rows, local_rows, 0)
            got = lax.dynamic_slice_in_dim(first, (1 - core) * local_rows, local_rows, 0)
            first = in_order(core, mine, lax.ppermute(got, "c", SWAP)).astype(jnp.float32)
            second = sum_lanes(contract(layer_at, part, other, masks[layer_at], late))
            total = jnp.concatenate([first, second], axis=2)
        else:
            total = sum_lanes(contract(layer_at, part, other, masks[layer_at], early, late))
        update = jnp.concatenate([total[0], total[1]], axis=1)
        residual = (residual.astype(jnp.float32) + update).astype(jnp.bfloat16)
    return residual


def solution(mesh):
    fine = Mesh(mesh.devices.reshape(2, 4, 2, 4, 2), ALL)
    split = P(ALL, None)
    return jax.shard_map(
        body, mesh=fine, in_specs=(split, P(), split, split, P()), out_specs=split, check_vma=False
    )
```

```python
import jax
import jax.numpy as jnp
from jax import lax
from jax.experimental import pallas as pl
from jax.experimental.pallas import tpu as pltpu
from jax.sharding import Mesh
from jax.sharding import PartitionSpec as P

BLOCK = 128
LAYERS = 2
HELD = 6
TILE = 1024
ALL = ("xh", "y", "xl", "z", "c")
ROW = ("xl", "z", "c")
SWAP = [(0, 1), (1, 0)]


def normalize(rows_in, gain_row):
    values = rows_in.astype(jnp.float32)
    row_mean = jnp.mean(values, axis=1, keepdims=True)
    centered = values - row_mean
    row_var = jnp.mean(centered * centered, axis=1, keepdims=True)
    return (centered * lax.rsqrt(row_var + 1e-05) * gain_row[None, :]).astype(jnp.bfloat16)


def pick_up(chosen, rows):
    groups, width = chosen.shape[0], rows.shape[1]

    def copy(chosen_ref, in_ref, out_ref):
        out_ref[0] = in_ref[...]

    return pl.pallas_call(
        copy,
        grid_spec=pltpu.PrefetchScalarGridSpec(
            num_scalar_prefetch=1,
            grid=(groups,),
            in_specs=[pl.BlockSpec((BLOCK, width), lambda g, ch: (ch[g], 0))],
            out_specs=pl.BlockSpec((1, BLOCK, width), lambda g, ch: (g, 0, 0)),
        ),
        out_shape=jax.ShapeDtypeStruct((groups, BLOCK, width), rows.dtype),
        compiler_params=pltpu.CompilerParams(vmem_limit_bytes=24 << 20),
        cost_estimate=pl.CostEstimate(flops=0, bytes_accessed=groups * BLOCK * width * 4, transcendentals=0),
        name="pick_up",
    )(chosen, rows)


def pick_down(table, rows, got, first, count):
    groups, tiles = (table.shape[0] - 1) // 2, got.shape[1] // TILE

    def copy(table_ref, own_ref, got_ref, out_ref):
        core = table_ref[2 * groups]
        out_ref[0, core] = own_ref[...]
        out_ref[0, 1 - core] = got_ref[...]

    return pl.pallas_call(
        copy,
        grid_spec=pltpu.PrefetchScalarGridSpec(
            num_scalar_prefetch=1,
            grid=(groups, count),
            in_specs=[
                pl.BlockSpec((BLOCK, TILE), lambda g, n, tb: (tb[g], tb[2 * groups] * tiles + first + n)),
                pl.BlockSpec((BLOCK, TILE), lambda g, n, tb: (tb[groups + g], first + n)),
            ],
            out_specs=pl.BlockSpec((1, 2, BLOCK, TILE), lambda g, n, tb: (g, 0, 0, n)),
        ),
        out_shape=jax.ShapeDtypeStruct((groups, 2, BLOCK, count * TILE), rows.dtype),
        compiler_params=pltpu.CompilerParams(vmem_limit_bytes=24 << 20),
        cost_estimate=pl.CostEstimate(flops=0, bytes_accessed=groups * BLOCK * count * TILE * 8, transcendentals=0),
        name="pick_down",
    )(table, rows, got)


def expand(core, layer_at, rows, up_own, up_got):
    slots = up_own.shape[0] // LAYERS
    count, half = rows.shape
    step = 2
    wide = step * BLOCK

    def kernel(core_ref, rows_ref, own_ref, got_ref, out_ref, send_ref):
        def product(ref):
            return lax.dot_general(
                rows_ref[...],
                ref[...].reshape(wide, half),
                (((1,), (1,)), ((), ())),
                preferred_element_type=jnp.float32,
            )

        at, done = core_ref[0], pl.program_id(0) * wide
        for unit, ref in ((at, own_ref), (1 - at, got_ref)):
            columns = pl.ds(pl.multiple_of(unit * slots * BLOCK + done, wide), wide)
            share = product(ref)
            out_ref[:, columns] = share
            send_ref[:, columns] = share.astype(jnp.bfloat16)

    first = layer_at * slots // step
    return pl.pallas_call(
        kernel,
        grid_spec=pltpu.PrefetchScalarGridSpec(
            num_scalar_prefetch=1,
            grid=(slots // step,),
            in_specs=[
                pl.BlockSpec((count, half), lambda s, at: (0, 0)),
                pl.BlockSpec((step, BLOCK, half), lambda s, at: (first + s, 0, at[0])),
                pl.BlockSpec((step, BLOCK, half), lambda s, at: (first + s, 0, 0)),
            ],
            out_specs=[pl.BlockSpec((count, slots * 2 * BLOCK), lambda s, at: (0, 0))] * 2,
        ),
        out_shape=[jax.ShapeDtypeStruct((count, slots * 2 * BLOCK), t) for t in (jnp.float32, jnp.bfloat16)],
        compiler_params=pltpu.CompilerParams(vmem_limit_bytes=32 << 20),
        cost_estimate=pl.CostEstimate(
            flops=4 * count * slots * BLOCK * half, bytes_accessed=slots * BLOCK * half * 4, transcendentals=0
        ),
        name="expand",
    )(core, rows, up_own, up_got)


def contract(layer_at, part, other, mask, *parts):
    tile = TILE if len(parts) == 1 else TILE // 2
    slots = parts[0].shape[0] // LAYERS
    count, hidden_units = part.shape
    per_unit = hidden_units // 2
    tiles = [array.shape[3] // tile for array in parts]
    starts = [sum(tiles[:i]) for i in range(len(tiles))]

    def kernel(part_ref, other_ref, mask_ref, *refs):
        down_refs, out_ref, active_ref = refs[: len(parts)], refs[-2], refs[-1]
        at = pl.program_id(0)

        @pl.when(at == 0)
        def _():
            pre_act = part_ref[...] + other_ref[...].astype(jnp.float32)
            active_ref[...] = (jnp.maximum(pre_act, 0.0) * mask_ref[...]).astype(jnp.bfloat16)

        for ref, start, number in zip(down_refs, starts, tiles):

            @pl.when((at >= start) & (at < start + number))
            def _(ref=ref):
                total = jnp.dot(
                    active_ref[:, :per_unit], ref[:, 0].reshape(per_unit, tile), preferred_element_type=jnp.float32
                )
                total += jnp.dot(
                    active_ref[:, per_unit:], ref[:, 1].reshape(per_unit, tile), preferred_element_type=jnp.float32
                )
                out_ref[...] = total.astype(jnp.bfloat16)

    def down_spec(start, number):
        return pl.BlockSpec(
            (slots, 2, BLOCK, tile), lambda n: (layer_at, 0, 0, jnp.clip(n - start, 0, number - 1))
        )

    return pl.pallas_call(
        kernel,
        grid=(sum(tiles),),
        in_specs=[
            pl.BlockSpec((count, hidden_units), lambda n: (0, 0)),
            pl.BlockSpec((count, hidden_units), lambda n: (0, 0)),
            pl.BlockSpec((1, hidden_units), lambda n: (0, 0)),
            *[down_spec(start, number) for start, number in zip(starts, tiles)],
        ],
        out_specs=pl.BlockSpec((count, tile), lambda n: (0, n)),
        out_shape=jax.ShapeDtypeStruct((count, sum(tiles) * tile), jnp.bfloat16),
        scratch_shapes=[pltpu.VMEM((count, hidden_units), jnp.bfloat16)],
        compiler_params=pltpu.CompilerParams(vmem_limit_bytes=32 << 20),
        cost_estimate=pl.CostEstimate(
            flops=2 * count * hidden_units * sum(tiles) * tile,
            bytes_accessed=hidden_units * sum(tiles) * tile * 2,
            transcendentals=0,
        ),
        name="contract",
    )(part, other, mask, *parts)


def sum_lanes(out):
    lanes, local_rows = 16, out.shape[0] // 16
    out = lax.all_to_all(out.reshape(lanes, local_rows, out.shape[1]), ROW, 0, 0, tiled=True)
    return jnp.sum(out.reshape(lanes // 2, 2, local_rows, -1).astype(jnp.float32), axis=0)


def in_order(core, mine, got):
    return jnp.where(core == 0, jnp.stack([mine, got]), jnp.stack([got, mine]))


def device(x, y, z, c):
    return (((x // 2 * 4 + y) * 2 + x % 2) * 4 + z) * 2 + c


def to_groups(blocks):
    sets = [
        [device(x, y, z, c) for x in pair for y in range(4)]
        for pair in ((0, 3), (1, 2))
        for z in range(4)
        for c in range(2)
    ]
    return lax.all_to_all(blocks, ALL, 0, 0, tiled=True, axis_index_groups=sets)


def body(hidden, gains, up_rows, down_rows, pick):
    owners, lanes = 8, 16
    owner = lax.axis_index(("xh", "y"))
    chip_lane = lax.axis_index(("xl", "z")) * 2
    core = lax.axis_index("c")
    local_rows, width = hidden.shape
    half = width // 2
    sent = jnp.minimum(lax.dynamic_slice_in_dim(pick, owner * lanes + chip_lane, 2, 1), HELD - 1)
    own_sent = lax.dynamic_index_in_dim(sent, core, 1, keepdims=False)
    other_sent = lax.dynamic_index_in_dim(sent, 1 - core, 1, keepdims=False)
    group_picks = lax.dynamic_slice_in_dim(pick, owner, 1, 0).reshape(LAYERS, owners // LAYERS, 2, 4, 2)
    side = lax.axis_index("xl") ^ lax.axis_index("xh")
    masks = []
    for layer_at in range(LAYERS):
        lane_picks = lax.dynamic_index_in_dim(group_picks[layer_at], side ^ layer_at, 1, keepdims=False)
        lane_picks = lax.dynamic_index_in_dim(lane_picks, lax.axis_index("z"), 1, keepdims=False)
        live = (lane_picks < HELD).astype(jnp.float32).T.reshape(-1)
        masks.append(jnp.repeat(live, BLOCK)[None, :])
    core_at = core.reshape(1)

    def other_half(array):
        return lax.dynamic_slice_in_dim(array, (1 - core) * half, half, array.ndim - 1)

    up_own = to_groups(pick_up(own_sent, up_rows))
    down_got = lax.ppermute(other_half(down_rows), "c", SWAP)
    table = jnp.concatenate([own_sent, other_sent, core_at])
    tiles = half // TILE
    early = to_groups(pick_down(table, down_rows, down_got, 0, tiles - 1))
    late = to_groups(pick_down(table, down_rows, down_got, tiles - 1, 1))
    up_got = lax.ppermute(other_half(up_own), "c", SWAP)

    residual = hidden
    for layer_at in range(LAYERS):
        normed = normalize(residual, gains[layer_at])
        if layer_at == 0:
            mine = lax.dynamic_slice_in_dim(normed, core * half, half, 1)
            got = lax.ppermute(other_half(normed), "c", SWAP)
            rows = lax.all_gather(in_order(core, mine, got).reshape(2 * local_rows, half), ("xl", "z"), axis=0, tiled=True)
        else:
            halves = jnp.stack([normed[:, :half], normed[:, half:]])
            spread = jnp.broadcast_to(halves[None], (lanes // 2, 2, local_rows, half))
            rows = lax.all_to_all(spread.reshape(lanes, local_rows, half), ROW, 0, 0, tiled=True)
            rows = rows.reshape(lanes * local_rows, half)
        part, sent_part = expand(core_at, layer_at, rows, up_own, up_got)
        other = lax.ppermute(sent_part, "c", SWAP)
        if layer_at == 0:
            first = contract(layer_at, part, other, masks[layer_at], early)
            first = lax.psum_scatter(first, ("xl", "z"), scatter_dimension=0, tiled=True)
            mine = lax.dynamic_slice_in_dim(first, core * local_rows, local_rows, 0)
            got = lax.dynamic_slice_in_dim(first, (1 - core) * local_rows, local_rows, 0)
            first = in_order(core, mine, lax.ppermute(got, "c", SWAP)).astype(jnp.float32)
            second = sum_lanes(contract(layer_at, part, other, masks[layer_at], late))
            total = jnp.concatenate([first, second], axis=2)
        else:
            total = sum_lanes(contract(layer_at, part, other, masks[layer_at], early, late))
        update = jnp.concatenate([total[0], total[1]], axis=1)
        residual = (residual.astype(jnp.float32) + update).astype(jnp.bfloat16)
    return residual


def solution(mesh):
    fine = Mesh(mesh.devices.reshape(2, 4, 2, 4, 2), ALL)
    split = P(ALL, None)
    return jax.shard_map(
        body, mesh=fine, in_specs=(split, P(), split, split, P()), out_specs=split, check_vma=False
    )
```
